32 devices in a mesh: groups: 2 (over x), rows: 4 (over y, core), cols: 4 (over z).
Axes of the slice: x: 2, y: 2, z: 4, core: 2. Of those that a mesh axis runs over, the one named last changes fastest.
Arguments:
- points: float32 [24, 13312], P(None, ('groups', 'rows', 'cols')), parts along dimension 1, may hold values from -6 to 6
- lengthscale: float32 [48], P('groups'), parts along dimension 0, may hold values from 1.5 to 6
- target: float32 [13312], P(('groups', 'rows', 'cols')), parts along dimension 0, may hold values from -6 to 6
- probes: int32 [7, 13312], P(None, ('groups', 'rows', 'cols')), parts along dimension 1, may hold values from 0 to 1
- noise: float32 [13312], P(('groups', 'rows', 'cols')), parts along dimension 0, may hold values from 0.05 to 0.5
Outputs:
- product: float32 [8, 13312], P(None, ('groups', 'rows', 'cols')), parts along dimension 1
The draws below stay inside these ranges and needn't reach their ends.
There are 2 independent parts, one for each index of `groups`. The reference program is written for one: setup_inputs(seed, part) draws one part's arguments, and reference() takes and returns one part's arrays. A program takes and returns all parts, laid end to end along the dimension named above; each array names one. Nothing has to cross between parts.
All inputs are finite; a program needn't handle non-finite values.
Results may differ from the reference program's by a relative error of at most 0.0085.
Values may be sent and summed in bfloat16 or wider, within the bound.
No kernel may reach another device: no remote copies, remote signals or barrier semaphores. Data moves between devices by JAX's collectives and lax.ppermute only.
A program may use at most 64 MiB of HBM per device.

```python
import math
import jax
import jax.numpy as jnp
from jax import lax

FEATURES = 24
VECTORS = 8
PROBES = 7
P_DEV = 416
POINTS = 6656


def with_ends(result, own_key, low, high):
    shape = result.shape
    place = [jax.random.randint(jax.random.fold_in(own_key, axis), (), 0, shape[axis]) for axis in range(len(shape))]
    result = result.at[tuple(place)].set(low)
    longest = shape.index(max(shape))
    place[longest] = (place[longest] + 1) % shape[longest]
    return result.at[tuple(place)].set(high)


def block_levels(own_key, extent, shards, low, largest):
    def one(axis_at, blocks):
        heights = jax.random.uniform(jax.random.fold_in(jax.random.fold_in(own_key, 6), axis_at), (blocks,), jnp.float32, low / len(shards), largest / len(shards))
        return jnp.repeat(jnp.exp(heights), extent[axis_at] // blocks).reshape((-1,) + (1,) * (len(extent) - axis_at - 1))

    factor_of = one(*shards[0])
    for cut in shards[1:]:
        factor_of = factor_of * one(*cut)
    return factor_of


def gaussian(rng, shape, width, reach, cuts=(), dtype=jnp.bfloat16):
    entries = jax.random.normal(rng, shape, jnp.float32) * width
    if len(cuts) > 0:
        entries = block_levels(rng, shape, cuts, -0.22, 0.18) * entries
    return jnp.clip(entries, min=-reach, max=reach).astype(dtype)


def setup_inputs(seed: int = 0, part: int = 0) -> dict:
    arg_keys = jax.random.split(jax.random.key(seed), 6)
    part_keys = jax.random.split(jax.random.fold_in(arg_keys[5], part), 6)
    points = gaussian(part_keys[0], (FEATURES, POINTS), 1.0, 6.0, ((1, 16),), jnp.float32)
    lengthscale = jnp.clip(jnp.exp(jax.random.uniform(part_keys[1], (FEATURES,), jnp.float32, math.log(1.5), math.log(6.0))), 1.5, 6.0)
    target = gaussian(part_keys[2], (POINTS,), 1.0, 6.0, ((0, 16),), jnp.float32)
    probes = with_ends(jax.random.randint(part_keys[3], (PROBES, POINTS), 0, 2), jax.random.fold_in(part_keys[3], 1), 0, 1).astype(jnp.int32)
    noise = jnp.clip(jnp.exp(math.log(0.5) - 2.3025851 * jax.random.uniform(part_keys[4], (POINTS,), jnp.float32) ** block_levels(part_keys[4], (POINTS,), ((0, 16),), -0.2, 0.2)), 0.05, 0.5)
    return dict(points=points, lengthscale=lengthscale, target=target, probes=probes, noise=noise)


def reference(points, lengthscale, target, probes, noise):
    scaled = (points / lengthscale[:, None]).astype(jnp.bfloat16)
    sqnorm = jnp.sum(scaled.astype(jnp.float32) ** 2, axis=0)
    signs = (2 * probes - 1).astype(jnp.float32)
    vectors = jnp.concatenate([target[None, :], signs], axis=0).astype(jnp.bfloat16)
    blocks = POINTS // P_DEV
    block_scaled = scaled.reshape(FEATURES, blocks, P_DEV).transpose(1, 0, 2)
    block_norm = sqnorm.reshape(blocks, P_DEV)

    def one_block(item):
        cols_scaled, cols_norm = item
        cross = lax.dot_general(scaled, cols_scaled, (((0,), (0,)), ((), ())), preferred_element_type=jnp.float32)
        dist = sqnorm[:, None] + cols_norm[None, :] - 2.0 * cross
        kernel = jnp.exp(-0.5 * dist).astype(jnp.bfloat16)
        return jnp.dot(vectors, kernel, preferred_element_type=jnp.float32)

    sums = lax.map(one_block, (block_scaled, block_norm))
    sums = sums.transpose(1, 0, 2).reshape(VECTORS, POINTS)
    return sums + noise[None, :] * vectors.astype(jnp.float32)
```

```python
import functools

import jax
import jax.numpy as jnp
from jax import lax
from jax.experimental import pallas as pl
from jax.experimental.pallas import tpu as pltpu
from jax.sharding import PartitionSpec as P

VMEM = pltpu.VMEM
IN_VMEM = pl.BlockSpec(memory_space=VMEM)


def near(x):
    return pltpu.with_memory_space_constraint(x, VMEM)


def prepare_kernel(points_ref, lengthscale_ref, target_ref, probes_ref, block_ref):
    features = points_ref.shape[0]
    wide = jnp.broadcast_to(lengthscale_ref[...], (features, features))
    row = lax.broadcasted_iota(jnp.int32, wide.shape, 0)
    col = lax.broadcasted_iota(jnp.int32, wide.shape, 1)
    scale = jnp.sum(jnp.where(row == col, wide, 0.0), axis=1, keepdims=True)
    scaled = points_ref[...] / scale
    signs = (2 * probes_ref[...] - 1).astype(jnp.float32)
    block = jnp.concatenate([scaled, target_ref[...], signs], axis=0)
    block_ref[...] = block.astype(jnp.bfloat16)


def augmented(block, features, own):
    x = block.astype(jnp.float32)
    row = lax.broadcasted_iota(jnp.int32, x.shape, 0)
    x = jnp.where(row < features, x, 0.0)
    half = -0.5 * jnp.sum(x * x, axis=0, keepdims=True)
    high = half.astype(jnp.bfloat16).astype(jnp.float32)
    rest = half - high
    middle = rest.astype(jnp.bfloat16).astype(jnp.float32)
    parts = [high, middle, rest - middle]
    rows = [1.0, 1.0, 1.0] + parts if own else parts + [1.0, 1.0, 1.0]
    for place, value in enumerate(rows):
        x = jnp.where(row == features + place, value, x)
    return x.astype(jnp.bfloat16)


def add_blocks(features, counts, last, *refs):
    piece_refs, rest = refs[: len(counts)], refs[len(counts) :]
    own_ref, rest = rest[0], rest[1:]
    noise_ref, rest = (rest[0], rest[1:]) if last else (None, rest)
    sum_ref, out_ref = rest if len(rest) == 2 else (None, rest[0])
    own = own_ref[...]
    own_side = augmented(own, features, True)
    blocks = [(ref, k) for ref, count in zip(piece_refs, counts) for k in range(count)]
    low = features // 16 * 16

    def exponent(ref, k):
        return lax.dot_general(
            augmented(ref[k], features, False),
            own_side,
            (((0,), (0,)), ((), ())),
            preferred_element_type=jnp.float32,
        )

    total = None
    ahead = exponent(*blocks[0])
    for at, (ref, k) in enumerate(blocks):
        now = ahead
        if at + 1 < len(blocks):
            ahead = exponent(*blocks[at + 1])
        kernel = jnp.exp(now).astype(jnp.bfloat16)
        term = jnp.dot(ref[k][low:], kernel, preferred_element_type=jnp.float32)
        total = term if total is None else total + term
    total = total[features - low :]
    if sum_ref is not None:
        total = total + sum_ref[...]
    if last:
        total = total + noise_ref[...] * own[features:].astype(jnp.float32)
    out_ref[...] = total


def add(features, pieces, own, noise=None, total=None):
    rows, width = own.shape
    counts = tuple(piece.shape[0] for piece in pieces)
    last = noise is not None
    operands = [near(piece) for piece in pieces] + [near(own)]
    if last:
        operands.append(noise)
    if total is not None:
        operands.append(near(total))
    shape = (rows - features, width)
    out = jax.ShapeDtypeStruct(shape, jnp.float32) if last else VMEM(shape, jnp.float32)
    work = sum(counts) * width * width
    return pl.pallas_call(
        functools.partial(add_blocks, features, counts, last),
        out_shape=out,
        in_specs=[IN_VMEM] * len(operands),
        out_specs=IN_VMEM,
        cost_estimate=pl.CostEstimate(flops=2 * work * 512, bytes_accessed=0, transcendentals=work),
    )(*operands)


def swap(x, mesh_shape, row_bits, col_bits):
    rows, cols = mesh_shape
    pairs = [
        (r * cols + c, (r ^ row_bits) * cols + (c ^ col_bits)) for r in range(rows) for c in range(cols)
    ]
    return lax.ppermute(x, ("rows", "cols"), pairs)


def powers(top):
    found = []
    while top > 1:
        top //= 2
        found.append(top)
    return found


def local(mesh_shape, points, lengthscale, target, probes, noise):
    features, width = points.shape
    rows, cols = mesh_shape
    vectors = probes.shape[0] + 1
    block = pl.pallas_call(
        prepare_kernel,
        out_shape=VMEM((features + vectors, width), jnp.bfloat16),
        in_specs=[IN_VMEM] * 4,
        out_specs=IN_VMEM,
    )(points, lengthscale[None, :], target[None, :], probes)
    mine = block[None]
    for bits in powers(cols):
        mine = jnp.concatenate([mine, swap(mine, mesh_shape, 1, bits)], axis=0)
    for bits in powers(rows)[:-1]:
        mine = jnp.concatenate([mine, swap(mine, mesh_shape, bits + 1, 0)], axis=0)
    other = swap(mine, mesh_shape, 1, 0)
    total = add(features, [mine], block)
    return add(features, [other], block, noise[None, :], total)


def solution(mesh):
    mesh_shape = (mesh.shape["rows"], mesh.shape["cols"])
    return jax.shard_map(
        functools.partial(local, mesh_shape),
        mesh=mesh,
        in_specs=(
            P(None, ("groups", "rows", "cols")),
            P("groups"),
            P(("groups", "rows", "cols")),
            P(None, ("groups", "rows", "cols")),
            P(("groups", "rows", "cols")),
        ),
        out_specs=P(None, ("groups", "rows", "cols")),
        check_vma=False,
    )
```

```python
import functools

import jax
import jax.numpy as jnp
from jax import lax
from jax.experimental import pallas as pl
from jax.experimental.pallas import tpu as pltpu
from jax.sharding import PartitionSpec as P

VMEM = pltpu.VMEM
IN_VMEM = pl.BlockSpec(memory_space=VMEM)


def near(x):
    return pltpu.with_memory_space_constraint(x, VMEM)


def prepare_kernel(points_ref, lengthscale_ref, target_ref, probes_ref, noise_ref, block_ref, base_ref):
    features = points_ref.shape[0]
    wide = jnp.broadcast_to(lengthscale_ref[...], (features, features))
    row = lax.broadcasted_iota(jnp.int32, wide.shape, 0)
    col = lax.broadcasted_iota(jnp.int32, wide.shape, 1)
    scale = jnp.sum(jnp.where(row == col, wide, 0.0), axis=1, keepdims=True)
    scaled = points_ref[...] / scale
    signs = (2 * probes_ref[...] - 1).astype(jnp.float32)
    block = jnp.concatenate([scaled, target_ref[...], signs], axis=0)
    block = block.astype(jnp.bfloat16)
    block_ref[...] = block
    base_ref[...] = noise_ref[...] * block[features:].astype(jnp.float32)


def augmented(block, features, own):
    x = block.astype(jnp.float32)
    row = lax.broadcasted_iota(jnp.int32, x.shape, 0)
    x = jnp.where(row < features, x, 0.0)
    half = -0.5 * jnp.sum(x * x, axis=0, keepdims=True)
    high = half.astype(jnp.bfloat16).astype(jnp.float32)
    rest = half - high
    middle = rest.astype(jnp.bfloat16).astype(jnp.float32)
    parts = [high, middle, rest - middle]
    rows = [1.0, 1.0, 1.0] + parts if own else parts + [1.0, 1.0, 1.0]
    for place, value in enumerate(rows):
        x = jnp.where(row == features + place, value, x)
    return x.astype(jnp.bfloat16)


def add_blocks(features, counts, *refs):
    piece_refs = refs[: len(counts)]
    own_ref, out_ref = refs[len(counts)], refs[-1]
    total = refs[len(counts) + 1][...] if len(refs) == len(counts) + 3 else None
    own_side = augmented(own_ref[...], features, True)
    blocks = [(ref, k) for ref, count in zip(piece_refs, counts) for k in range(count)]
    low = features // 16 * 16

    def exponent(ref, k):
        return lax.dot_general(
            augmented(ref[k], features, False),
            own_side,
            (((0,), (0,)), ((), ())),
            preferred_element_type=jnp.float32,
        )

    found = None
    ahead = exponent(*blocks[0])
    for at, (ref, k) in enumerate(blocks):
        now = ahead
        if at + 1 < len(blocks):
            ahead = exponent(*blocks[at + 1])
        kernel = jnp.exp(now).astype(jnp.bfloat16)
        term = jnp.dot(ref[k][low:], kernel, preferred_element_type=jnp.float32)
        found = term if found is None else found + term
    found = found[features - low :]
    out_ref[...] = found if total is None else total + found


def add(features, pieces, own, total=None):
    rows, width = own.shape
    counts = tuple(piece.shape[0] for piece in pieces)
    operands = [near(x) for x in (*pieces, own, total) if x is not None]
    shape = (rows - features, width)
    out = VMEM(shape, jnp.float32)
    work = sum(counts) * width * width
    return pl.pallas_call(
        functools.partial(add_blocks, features, counts),
        out_shape=out,
        in_specs=[IN_VMEM] * len(operands),
        out_specs=IN_VMEM,
        cost_estimate=pl.CostEstimate(flops=20 * work * 512, bytes_accessed=0, transcendentals=work),
    )(*operands)


def swap(x, mesh_shape, row_bits, col_bits):
    rows, cols = mesh_shape
    pairs = [
        (r * cols + c, (r ^ row_bits) * cols + (c ^ col_bits)) for r in range(rows) for c in range(cols)
    ]
    return lax.ppermute(x, ("rows", "cols"), pairs)


def powers(top):
    found = []
    while top > 1:
        top //= 2
        found.append(top)
    return found


def local(mesh_shape, points, lengthscale, target, probes, noise):
    features, width = points.shape
    rows, cols = mesh_shape
    vectors = probes.shape[0] + 1
    block, base = pl.pallas_call(
        prepare_kernel,
        out_shape=(VMEM((features + vectors, width), jnp.bfloat16), VMEM((vectors, width), jnp.float32)),
        in_specs=[IN_VMEM] * 5,
        out_specs=(IN_VMEM, IN_VMEM),
    )(points, lengthscale[None, :], target[None, :], probes, noise[None, :])
    peer = swap(block, mesh_shape, 3, 0)
    mine = block[None]
    for bits in powers(cols):
        mine = jnp.concatenate([mine, swap(mine, mesh_shape, 1, bits)], axis=0)
    for bits in powers(rows)[:-2]:
        mine = jnp.concatenate([mine, swap(mine, mesh_shape, bits + 1, 0)], axis=0)
    other = swap(mine, mesh_shape, 1, 0)
    partial = add(features, [mine], peer)
    partial = add(features, [other], peer, partial)
    total = add(features, [mine, other], block, base)
    return total + swap(partial, mesh_shape, 3, 0)


def solution(mesh):
    mesh_shape = (mesh.shape["rows"], mesh.shape["cols"])
    return jax.shard_map(
        functools.partial(local, mesh_shape),
        mesh=mesh,
        in_specs=(
            P(None, ("groups", "rows", "cols")),
            P("groups"),
            P(("groups", "rows", "cols")),
            P(None, ("groups", "rows", "cols")),
            P(("groups", "rows", "cols")),
        ),
        out_specs=P(None, ("groups", "rows", "cols")),
        check_vma=False,
    )
```

```python
import functools

import jax
import jax.numpy as jnp
from jax import lax
from jax.experimental import pallas as pl
from jax.experimental.pallas import tpu as pltpu
from jax.sharding import PartitionSpec as P

VMEM = pltpu.VMEM
IN_VMEM = pl.BlockSpec(memory_space=VMEM)
CHUNK = 256
AHEAD = 2


def near(x):
    return pltpu.with_memory_space_constraint(x, VMEM)


def prepare_kernel(points_ref, lengthscale_ref, target_ref, probes_ref, noise_ref, block_ref, base_ref):
    features = points_ref.shape[0]
    wide = jnp.broadcast_to(lengthscale_ref[...], (features, features))
    row = lax.broadcasted_iota(jnp.int32, wide.shape, 0)
    col = lax.broadcasted_iota(jnp.int32, wide.shape, 1)
    scale = jnp.sum(jnp.where(row == col, wide, 0.0), axis=1, keepdims=True)
    scaled = points_ref[...] / scale
    signs = (2 * probes_ref[...] - 1).astype(jnp.float32)
    block = jnp.concatenate([scaled, target_ref[...], signs], axis=0)
    block = block.astype(jnp.bfloat16)
    block_ref[...] = block
    base_ref[...] = noise_ref[...] * block[features:].astype(jnp.float32)


def augmented(block, features, own):
    x = block.astype(jnp.float32)
    row = lax.broadcasted_iota(jnp.int32, x.shape, 0)
    x = jnp.where(row < features, x, 0.0)
    half = -0.5 * jnp.sum(x * x, axis=0, keepdims=True)
    high = half.astype(jnp.bfloat16).astype(jnp.float32)
    rest = half - high
    middle = rest.astype(jnp.bfloat16).astype(jnp.float32)
    parts = [high, middle, rest - middle]
    rows = [1.0, 1.0, 1.0] + parts if own else parts + [1.0, 1.0, 1.0]
    for place, value in enumerate(rows):
        x = jnp.where(row == features + place, value, x)
    return x.astype(jnp.bfloat16)


def add_blocks(features, counts, *refs):
    piece_refs = refs[: len(counts)]
    own_ref, out_ref = refs[len(counts)], refs[-1]
    total = refs[len(counts) + 1][...] if len(refs) == len(counts) + 3 else None
    own_side = augmented(own_ref[...], features, True)
    width = own_ref.shape[1]
    low = features // 16 * 16
    blocks = [(ref, k) for ref, count in zip(piece_refs, counts) for k in range(count)]
    chunks = [(at, lo, min(lo + CHUNK, width)) for at in range(len(blocks)) for lo in range(0, width, CHUNK)]
    sides = {}

    def exponent(at, lo, hi):
        if at not in sides:
            ref, k = blocks[at]
            sides[at] = augmented(ref[k], features, False)
        return lax.dot_general(
            sides[at][:, lo:hi], own_side, (((0,), (0,)), ((), ())), preferred_element_type=jnp.float32
        )

    found = None
    ahead = [exponent(*chunk) for chunk in chunks[:AHEAD]]
    for step, (at, lo, hi) in enumerate(chunks):
        now = ahead.pop(0)
        if step + AHEAD < len(chunks):
            ahead.append(exponent(*chunks[step + AHEAD]))
        kernel = jnp.exp(now).astype(jnp.bfloat16)
        ref, k = blocks[at]
        term = jnp.dot(ref[k][low:, lo:hi], kernel, preferred_element_type=jnp.float32)
        found = term if found is None else found + term
    found = found[features - low :]
    out_ref[...] = found if total is None else total + found


def add(features, pieces, own, total=None):
    rows, width = own.shape
    counts = tuple(piece.shape[0] for piece in pieces)
    operands = [near(x) for x in (*pieces, own, total) if x is not None]
    shape = (rows - features, width)
    out = VMEM(shape, jnp.float32)
    work = sum(counts) * width * width
    return pl.pallas_call(
        functools.partial(add_blocks, features, counts),
        out_shape=out,
        in_specs=[IN_VMEM] * len(operands),
        out_specs=IN_VMEM,
        cost_estimate=pl.CostEstimate(flops=20 * work * 512, bytes_accessed=0, transcendentals=work),
    )(*operands)


def swap(x, mesh_shape, row_bits, col_bits):
    rows, cols = mesh_shape
    pairs = [
        (r * cols + c, (r ^ row_bits) * cols + (c ^ col_bits)) for r in range(rows) for c in range(cols)
    ]
    return lax.ppermute(x, ("rows", "cols"), pairs)


def powers(top):
    found = []
    while top > 1:
        top //= 2
        found.append(top)
    return found


def local(mesh_shape, points, lengthscale, target, probes, noise):
    features, width = points.shape
    rows, cols = mesh_shape
    vectors = probes.shape[0] + 1
    block, base = pl.pallas_call(
        prepare_kernel,
        out_shape=(VMEM((features + vectors, width), jnp.bfloat16), VMEM((vectors, width), jnp.float32)),
        in_specs=[IN_VMEM] * 5,
        out_specs=(IN_VMEM, IN_VMEM),
    )(points, lengthscale[None, :], target[None, :], probes, noise[None, :])
    steps = [(1, bits) for bits in powers(cols)] + [(bits + 1, 0) for bits in powers(rows)[:-2]]
    peer = swap(block, mesh_shape, 3, 0)
    early = block[None]
    for step in steps[:-1]:
        early = jnp.concatenate([early, swap(early, mesh_shape, *step)], axis=0)
    late = swap(early, mesh_shape, *steps[-1])
    partial = add(features, [early], peer)
    sent, partial = lax.optimization_barrier((early, partial))
    early_other = swap(sent, mesh_shape, 1, 0)
    late_other = swap(late, mesh_shape, 1, 0)
    partial = add(features, [early_other, late], peer, partial)
    partial = add(features, [late_other], peer, partial)
    total = add(features, [early, early_other, late, late_other], block, base)
    return total + swap(partial, mesh_shape, 3, 0)


def solution(mesh):
    mesh_shape = (mesh.shape["rows"], mesh.shape["cols"])
    return jax.shard_map(
        functools.partial(local, mesh_shape),
        mesh=mesh,
        in_specs=(
            P(None, ("groups", "rows", "cols")),
            P("groups"),
            P(("groups", "rows", "cols")),
            P(None, ("groups", "rows", "cols")),
            P(("groups", "rows", "cols")),
        ),
        out_specs=P(None, ("groups", "rows", "cols")),
        check_vma=False,
    )
```

```python
import functools

import jax
import jax.numpy as jnp
from jax import lax
from jax.experimental import pallas as pl
from jax.experimental.pallas import tpu as pltpu
from jax.sharding import PartitionSpec as P

VMEM = pltpu.VMEM
IN_VMEM = pl.BlockSpec(memory_space=VMEM)
LANES = 128
CHUNK = 2
AHEAD = 2


def near(x):
    return pltpu.with_memory_space_constraint(x, VMEM)


def prepare_kernel(points_ref, lengthscale_ref, target_ref, probes_ref, noise_ref, block_ref, base_ref, packed_ref):
    features = points_ref.shape[0]
    wide = jnp.broadcast_to(lengthscale_ref[...], (features, features))
    row = lax.broadcasted_iota(jnp.int32, wide.shape, 0)
    col = lax.broadcasted_iota(jnp.int32, wide.shape, 1)
    scale = jnp.sum(jnp.where(row == col, wide, 0.0), axis=1, keepdims=True)
    scaled = points_ref[...] / scale
    signs = (2 * probes_ref[...] - 1).astype(jnp.float32)
    block = jnp.concatenate([scaled, target_ref[...], signs], axis=0)
    rows, width = block.shape
    full = width // LANES * LANES
    for tile in range(full // LANES):
        packed_ref[rows * tile : rows * (tile + 1), :] = block[:, LANES * tile : LANES * (tile + 1)].astype(jnp.bfloat16)
    high, low = block[: rows // 2, full:], block[rows // 2 :, full:]
    packed_ref[full // LANES * rows :, :] = jnp.concatenate([high, low, high, low], axis=1).astype(jnp.bfloat16)
    block = block.astype(jnp.bfloat16)
    block_ref[...] = block
    base_ref[...] = noise_ref[...] * block[features:].astype(jnp.float32)


def augmented(block, features, own):
    x = block.astype(jnp.float32)
    row = lax.broadcasted_iota(jnp.int32, x.shape, 0)
    x = jnp.where(row < features, x, 0.0)
    half = -0.5 * jnp.sum(x * x, axis=0, keepdims=True)
    high = half.astype(jnp.bfloat16).astype(jnp.float32)
    rest = half - high
    middle = rest.astype(jnp.bfloat16).astype(jnp.float32)
    parts = [high, middle, rest - middle]
    rows = [1.0, 1.0, 1.0] + parts if own else parts + [1.0, 1.0, 1.0]
    for place, value in enumerate(rows):
        x = jnp.where(row == features + place, value, x)
    return x.astype(jnp.bfloat16)


def rest_tile(first, second, features):
    rows = first.shape[0]
    first = first.astype(jnp.float32)
    lane = lax.broadcasted_iota(jnp.int32, (rows, LANES), 1)
    left = lane % (LANES // 2) < LANES // 4
    high, low = first, pltpu.roll(first, LANES - LANES // 4, 1)
    if second is None:
        row = lax.broadcasted_iota(jnp.int32, (rows, LANES), 0)
        low = jnp.where(left | (row + rows < features), low, 0.0)
    else:
        second = second.astype(jnp.float32)
        high = jnp.where(left, high, pltpu.roll(second, LANES // 4, 1))
        low = jnp.where(left, low, second)
    return jnp.concatenate([high, low], axis=0).astype(jnp.bfloat16)


def add_pieces(features, counts, *refs):
    piece_refs = refs[: len(counts)]
    own_ref, out_ref = refs[len(counts)], refs[-1]
    total = refs[len(counts) + 1][...] if len(refs) == len(counts) + 3 else None
    own_side = augmented(own_ref[...], features, True)
    rows = own_ref.shape[0]
    low = features // 16 * 16
    pieces = [(ref, k) for ref, count in zip(piece_refs, counts) for k in range(count)]
    whole = piece_refs[0].shape[1] // rows * rows
    tiles = [(ref, k, lo) for ref, k in pieces for lo in range(0, whole, rows)]
    tiles += [(pieces[at : at + 2],) for at in range(0, len(pieces), 2)]
    chunks = [tiles[at : at + CHUNK] for at in range(0, len(tiles), CHUNK)]

    def load(tile):
        if len(tile) == 3:
            ref, k, lo = tile
            return ref[k, lo : lo + rows, :]
        both = [ref[k, whole:, :] for ref, k in tile[0]]
        return rest_tile(both[0], both[1] if len(both) == 2 else None, features)

    def exponent(chunk):
        block = jnp.concatenate([load(tile) for tile in chunk], axis=1)
        side = augmented(block, features, False)
        return block[low:], lax.dot_general(
            side, own_side, (((0,), (0,)), ((), ())), preferred_element_type=jnp.float32
        )

    found = total
    ahead = [exponent(chunk) for chunk in chunks[:AHEAD]]
    for step in range(len(chunks)):
        vectors, now = ahead.pop(0)
        if step + AHEAD < len(chunks):
            ahead.append(exponent(chunks[step + AHEAD]))
        kernel = jnp.exp(now).astype(jnp.bfloat16)
        term = jnp.dot(vectors, kernel, preferred_element_type=jnp.float32)
        term = term[features - low :]
        found = term if found is None else found + term
    out_ref[...] = found


def add(features, pieces, own, total=None):
    rows, width = own.shape
    counts = tuple(piece.shape[0] for piece in pieces)
    operands = [near(x) for x in (*pieces, own, total) if x is not None]
    shape = (rows - features, width)
    out = VMEM(shape, jnp.float32)
    work = 2 * sum(counts) * width * width
    return pl.pallas_call(
        functools.partial(add_pieces, features, counts),
        out_shape=out,
        in_specs=[IN_VMEM] * len(operands),
        out_specs=IN_VMEM,
        cost_estimate=pl.CostEstimate(flops=20 * work * 512, bytes_accessed=0, transcendentals=work),
    )(*operands)


def paired(first, second):
    whole = first.shape[0] // 32 * 32
    lane = lax.broadcasted_iota(jnp.int32, first[whole:].shape, 1)
    rest = jnp.where(lane < LANES // 2, first[whole:], second[whole:])
    return jnp.concatenate([first[:whole], second[:whole], rest], axis=0)[None]


def swap(x, mesh_shape, row_bits, col_bits):
    rows, cols = mesh_shape
    pairs = [
        (r * cols + c, (r ^ row_bits) * cols + (c ^ col_bits)) for r in range(rows) for c in range(cols)
    ]
    return lax.ppermute(x, ("rows", "cols"), pairs)


def powers(top):
    found = []
    while top > 1:
        top //= 2
        found.append(top)
    return found


def local(mesh_shape, points, lengthscale, target, probes, noise):
    features, width = points.shape
    rows, cols = mesh_shape
    vectors = probes.shape[0] + 1
    height = features + vectors
    packed_rows = width // LANES * height + height // 2
    block, base, packed = pl.pallas_call(
        prepare_kernel,
        out_shape=(
            VMEM((height, width), jnp.bfloat16),
            VMEM((vectors, width), jnp.float32),
            VMEM((packed_rows, LANES), jnp.bfloat16),
        ),
        in_specs=[IN_VMEM] * 5,
        out_specs=(IN_VMEM,) * 3,
    )(points, lengthscale[None, :], target[None, :], probes, noise[None, :])
    steps = [(1, bits) for bits in powers(cols)] + [(bits + 1, 0) for bits in powers(rows)[:-2]]
    peer = swap(block, mesh_shape, 3, 0)
    early = paired(packed, swap(packed, mesh_shape, *steps[0]))
    for step in steps[1:-1]:
        early = jnp.concatenate([early, swap(early, mesh_shape, *step)], axis=0)
    late = swap(early, mesh_shape, *steps[-1])
    partial = add(features, [early], peer)
    sent, partial = lax.optimization_barrier((early, partial))
    early_other = swap(sent, mesh_shape, 1, 0)
    late_other = swap(late, mesh_shape, 1, 0)
    partial = add(features, [early_other, late], peer, partial)
    partial = add(features, [late_other], peer, partial)
    total = add(features, [early, early_other, late, late_other], block, base)
    return total + swap(partial, mesh_shape, 3, 0)


def solution(mesh):
    mesh_shape = (mesh.shape["rows"], mesh.shape["cols"])
    return jax.shard_map(
        functools.partial(local, mesh_shape),
        mesh=mesh,
        in_specs=(
            P(None, ("groups", "rows", "cols")),
            P("groups"),
            P(("groups", "rows", "cols")),
            P(None, ("groups", "rows", "cols")),
            P(("groups", "rows", "cols")),
        ),
        out_specs=P(None, ("groups", "rows", "cols")),
        check_vma=False,
    )
```

```python
import functools

import jax
import jax.numpy as jnp
from jax import lax
from jax.experimental import pallas as pl
from jax.experimental.pallas import tpu as pltpu
from jax.sharding import PartitionSpec as P

VMEM = pltpu.VMEM
IN_VMEM = pl.BlockSpec(memory_space=VMEM)
LANES = 128
CHUNK = 2
AHEAD = 2


def near(x):
    return pltpu.with_memory_space_constraint(x, VMEM)


def prepare_kernel(points_ref, lengthscale_ref, target_ref, probes_ref, noise_ref, block_ref, base_ref, packed_ref):
    features = points_ref.shape[0]
    wide = jnp.broadcast_to(lengthscale_ref[...], (features, features))
    row = lax.broadcasted_iota(jnp.int32, wide.shape, 0)
    col = lax.broadcasted_iota(jnp.int32, wide.shape, 1)
    scale = jnp.sum(jnp.where(row == col, wide, 0.0), axis=1, keepdims=True)
    scaled = points_ref[...] / scale
    signs = (2 * probes_ref[...] - 1).astype(jnp.float32)
    block = jnp.concatenate([scaled, target_ref[...], signs], axis=0)
    rows, width = block.shape
    full = width // LANES * LANES
    for tile in range(full // LANES):
        packed_ref[rows * tile : rows * (tile + 1), :] = block[:, LANES * tile : LANES * (tile + 1)].astype(jnp.bfloat16)
    high, low = block[: rows // 2, full:], block[rows // 2 :, full:]
    packed_ref[full // LANES * rows :, :] = jnp.concatenate([high, low, high, low], axis=1).astype(jnp.bfloat16)
    block = block.astype(jnp.bfloat16)
    block_ref[...] = block
    base_ref[...] = noise_ref[...] * block[features:].astype(jnp.float32)


def augmented(block, features, own):
    x = block.astype(jnp.float32)
    row = lax.broadcasted_iota(jnp.int32, x.shape, 0)
    x = jnp.where(row < features, x, 0.0)
    half = -0.5 * jnp.sum(x * x, axis=0, keepdims=True)
    high = half.astype(jnp.bfloat16).astype(jnp.float32)
    rest = half - high
    middle = rest.astype(jnp.bfloat16).astype(jnp.float32)
    parts = [high, middle, rest - middle]
    rows = [1.0, 1.0, 1.0] + parts if own else parts + [1.0, 1.0, 1.0]
    for place, value in enumerate(rows):
        x = jnp.where(row == features + place, value, x)
    return x.astype(jnp.bfloat16)


def rest_tile(rests, features):
    quarter = LANES // 4
    rows = rests[0].shape[0]
    rests = [rest.astype(jnp.float32) for rest in rests]
    place = lax.broadcasted_iota(jnp.int32, (rows, LANES), 1) // quarter
    halves = [
        rests[at] if at + 1 >= len(rests) else jnp.where(place < 2, rests[at], rests[at + 1])
        for at in range(0, len(rests), 2)
    ]
    high, low = halves[0], pltpu.roll(halves[0], LANES - quarter, 1)
    if len(halves) == 2:
        high = jnp.where(place % 2 == 0, high, pltpu.roll(halves[1], quarter, 1))
        low = jnp.where(place % 2 == 0, low, halves[1])
    row = rows + lax.broadcasted_iota(jnp.int32, (rows, LANES), 0)
    for at, spot in enumerate((0, 2, 1, 3)):
        if at >= len(rests):
            low = jnp.where((place == spot) & (row >= features), 0.0, low)
    return jnp.concatenate([high, low], axis=0).astype(jnp.bfloat16)


def add_blocks(features, counts, *refs):
    piece_refs = refs[: len(counts)]
    own_ref, out_ref = refs[len(counts)], refs[-1]
    total = refs[len(counts) + 1][...] if len(refs) == len(counts) + 3 else None
    own_side = augmented(own_ref[...], features, True)
    rows = own_ref.shape[0]
    low = features // 16 * 16
    blocks = [(ref, k) for ref, count in zip(piece_refs, counts) for k in range(count)]
    whole = piece_refs[0].shape[1] // rows * rows
    tiles = [(ref, k, lo) for ref, k in blocks for lo in range(0, whole, rows)]
    tiles += [(blocks[at : at + 4],) for at in range(0, len(blocks), 4)]
    chunks = [tiles[at : at + CHUNK] for at in range(0, len(tiles), CHUNK)]

    def load(tile):
        if len(tile) == 3:
            ref, k, lo = tile
            return ref[k, lo : lo + rows, :]
        return rest_tile([ref[k, whole:, :] for ref, k in tile[0]], features)

    def exponent(chunk):
        block = jnp.concatenate([load(tile) for tile in chunk], axis=1)
        side = augmented(block, features, False)
        return block[low:], lax.dot_general(
            side, own_side, (((0,), (0,)), ((), ())), preferred_element_type=jnp.float32
        )

    found = total
    ahead = [exponent(chunk) for chunk in chunks[:AHEAD]]
    for step in range(len(chunks)):
        vectors, now = ahead.pop(0)
        if step + AHEAD < len(chunks):
            ahead.append(exponent(chunks[step + AHEAD]))
        kernel = jnp.exp(now).astype(jnp.bfloat16)
        term = jnp.dot(vectors, kernel, preferred_element_type=jnp.float32)
        term = term[features - low :]
        found = term if found is None else found + term
    out_ref[...] = found


def add(features, pieces, own, total=None):
    rows, width = own.shape
    counts = tuple(piece.shape[0] for piece in pieces)
    operands = [near(x) for x in (*pieces, own, total) if x is not None]
    shape = (rows - features, width)
    out = VMEM(shape, jnp.float32)
    work = sum(counts) * width * width
    return pl.pallas_call(
        functools.partial(add_blocks, features, counts),
        out_shape=out,
        in_specs=[IN_VMEM] * len(operands),
        out_specs=IN_VMEM,
        cost_estimate=pl.CostEstimate(flops=20480 * work, bytes_accessed=0, transcendentals=work),
    )(*operands)


def swap(x, mesh_shape, row_bits, col_bits):
    rows, cols = mesh_shape
    pairs = [
        (r * cols + c, (r ^ row_bits) * cols + (c ^ col_bits)) for r in range(rows) for c in range(cols)
    ]
    return lax.ppermute(x, ("rows", "cols"), pairs)


def powers(top):
    found = []
    while top > 1:
        top //= 2
        found.append(top)
    return found


def local(mesh_shape, points, lengthscale, target, probes, noise):
    features, width = points.shape
    rows, cols = mesh_shape
    vectors = probes.shape[0] + 1
    height = features + vectors
    packed_rows = width // LANES * height + height // 2
    block, base, packed = pl.pallas_call(
        prepare_kernel,
        out_shape=(
            VMEM((height, width), jnp.bfloat16),
            VMEM((vectors, width), jnp.float32),
            VMEM((packed_rows, LANES), jnp.bfloat16),
        ),
        in_specs=[IN_VMEM] * 5,
        out_specs=(IN_VMEM,) * 3,
    )(points, lengthscale[None, :], target[None, :], probes, noise[None, :])
    one = packed[None]
    for step in [(1, bits) for bits in powers(cols)[:-2]] + [(bits + 1, 0) for bits in powers(rows)[:-2]]:
        one = jnp.concatenate([one, swap(one, mesh_shape, *step)], axis=0)
    peer = swap(block, mesh_shape, 3, 0)
    next_to, second, far = (swap(one, mesh_shape, 1, bits) for bits in (1, 2, 3))
    early = jnp.concatenate([one, far], axis=0)
    late = jnp.concatenate([next_to, second], axis=0)
    total = add(features, [early], block, base)
    sent, total = lax.optimization_barrier((early, total))
    early_other = swap(sent, mesh_shape, 1, 0)
    late_other = swap(late, mesh_shape, 1, 0)
    partial = add(features, [early, early_other, late], peer)
    partial = add(features, [late_other], peer, partial)
    total = add(features, [early_other, late, late_other], block, total)
    return total + swap(partial, mesh_shape, 3, 0)


def solution(mesh):
    mesh_shape = (mesh.shape["rows"], mesh.shape["cols"])
    return jax.shard_map(
        functools.partial(local, mesh_shape),
        mesh=mesh,
        in_specs=(
            P(None, ("groups", "rows", "cols")),
            P("groups"),
            P(("groups", "rows", "cols")),
            P(None, ("groups", "rows", "cols")),
            P(("groups", "rows", "cols")),
        ),
        out_specs=P(None, ("groups", "rows", "cols")),
        check_vma=False,
    )
```

```python
import functools

import jax
import jax.numpy as jnp
from jax import lax
from jax.experimental import pallas as pl
from jax.experimental.pallas import tpu as pltpu
from jax.sharding import PartitionSpec as P

VMEM = pltpu.VMEM
IN_VMEM = pl.BlockSpec(memory_space=VMEM)
LANES = 128
CHUNK = 2
AHEAD = 2


def near(x):
    return pltpu.with_memory_space_constraint(x, VMEM)


def prepare_kernel(points_ref, lengthscale_ref, target_ref, probes_ref, noise_ref, block_ref, base_ref, packed_ref):
    features = points_ref.shape[0]
    wide = jnp.broadcast_to(lengthscale_ref[...], (features, features))
    row = lax.broadcasted_iota(jnp.int32, wide.shape, 0)
    col = lax.broadcasted_iota(jnp.int32, wide.shape, 1)
    scale = jnp.sum(jnp.where(row == col, wide, 0.0), axis=1, keepdims=True)
    scaled = points_ref[...] / scale
    signs = (2 * probes_ref[...] - 1).astype(jnp.float32)
    block = jnp.concatenate([scaled, target_ref[...], signs], axis=0)
    rows, width = block.shape
    full = width // LANES * LANES
    for tile in range(full // LANES):
        packed_ref[rows * tile : rows * (tile + 1), :] = block[:, LANES * tile : LANES * (tile + 1)].astype(jnp.bfloat16)
    high, low = block[: rows // 2, full:], block[rows // 2 :, full:]
    packed_ref[full // LANES * rows :, :] = jnp.concatenate([high, low, high, low], axis=1).astype(jnp.bfloat16)
    block = block.astype(jnp.bfloat16)
    block_ref[...] = block
    base_ref[...] = noise_ref[...] * block[features:].astype(jnp.float32)


def augmented(block, features, own):
    x = block.astype(jnp.float32)
    row = lax.broadcasted_iota(jnp.int32, x.shape, 0)
    x = jnp.where(row < features, x, 0.0)
    half = -0.5 * jnp.sum(x * x, axis=0, keepdims=True)
    high = half.astype(jnp.bfloat16).astype(jnp.float32)
    rest = half - high
    middle = rest.astype(jnp.bfloat16).astype(jnp.float32)
    parts = [high, middle, rest - middle]
    rows = [1.0, 1.0, 1.0] + parts if own else parts + [1.0, 1.0, 1.0]
    for place, value in enumerate(rows):
        x = jnp.where(row == features + place, value, x)
    return x.astype(jnp.bfloat16)


def rest_tile(rests, features):
    quarter = LANES // 4
    rows = rests[0].shape[0]
    rests = [rest.astype(jnp.float32) for rest in rests]
    place = lax.broadcasted_iota(jnp.int32, (rows, LANES), 1) // quarter
    halves = [
        rests[at] if at + 1 >= len(rests) else jnp.where(place < 2, rests[at], rests[at + 1])
        for at in range(0, len(rests), 2)
    ]
    high, low = halves[0], pltpu.roll(halves[0], LANES - quarter, 1)
    if len(halves) == 2:
        high = jnp.where(place % 2 == 0, high, pltpu.roll(halves[1], quarter, 1))
        low = jnp.where(place % 2 == 0, low, halves[1])
    row = rows + lax.broadcasted_iota(jnp.int32, (rows, LANES), 0)
    for at, spot in enumerate((0, 2, 1, 3)):
        if at >= len(rests):
            low = jnp.where((place == spot) & (row >= features), 0.0, low)
    return jnp.concatenate([high, low], axis=0).astype(jnp.bfloat16)


def add_blocks(features, counts, *refs):
    piece_refs = refs[: len(counts)]
    own_ref, out_ref = refs[len(counts)], refs[-1]
    total = refs[len(counts) + 1][...] if len(refs) == len(counts) + 3 else None
    own_side = augmented(own_ref[...], features, True)
    rows = own_ref.shape[0]
    low = features // 16 * 16
    blocks = [(ref, k) for ref, count in zip(piece_refs, counts) for k in range(count)]
    whole = piece_refs[0].shape[1] // rows * rows
    tiles = [(ref, k, lo) for ref, k in blocks for lo in range(0, whole, rows)]
    tiles += [(blocks[at : at + 4],) for at in range(0, len(blocks), 4)]
    chunks = [tiles[at : at + CHUNK] for at in range(0, len(tiles), CHUNK)]

    def load(tile):
        if len(tile) == 3:
            ref, k, lo = tile
            return ref[k, lo : lo + rows, :]
        return rest_tile([ref[k, whole:, :] for ref, k in tile[0]], features)

    def exponent(chunk):
        block = jnp.concatenate([load(tile) for tile in chunk], axis=1)
        side = augmented(block, features, False)
        return block[low:], lax.dot_general(
            side, own_side, (((0,), (0,)), ((), ())), preferred_element_type=jnp.float32
        )

    found = total
    ahead = [exponent(chunk) for chunk in chunks[:AHEAD]]
    for step in range(len(chunks)):
        vectors, now = ahead.pop(0)
        if step + AHEAD < len(chunks):
            ahead.append(exponent(chunks[step + AHEAD]))
        kernel = jnp.exp(now).astype(jnp.bfloat16)
        term = jnp.dot(vectors, kernel, preferred_element_type=jnp.float32)
        term = term[features - low :]
        found = term if found is None else found + term
    out_ref[...] = found


def add(features, pieces, own, total=None):
    rows, width = own.shape
    counts = tuple(piece.shape[0] for piece in pieces)
    operands = [near(x) for x in (*pieces, own, total) if x is not None]
    shape = (rows - features, width)
    out = VMEM(shape, jnp.float32)
    work = sum(counts) * width * width
    return pl.pallas_call(
        functools.partial(add_blocks, features, counts),
        out_shape=out,
        in_specs=[IN_VMEM] * len(operands),
        out_specs=IN_VMEM,
        cost_estimate=pl.CostEstimate(flops=20480 * work, bytes_accessed=0, transcendentals=work),
    )(*operands)


def swap(x, mesh_shape, row_bits, col_bits):
    rows, cols = mesh_shape
    pairs = [
        (r * cols + c, (r ^ row_bits) * cols + (c ^ col_bits)) for r in range(rows) for c in range(cols)
    ]
    return lax.ppermute(x, ("rows", "cols"), pairs)


def turn(x, mesh_shape, row_bits, places):
    rows, cols = mesh_shape
    pairs = [
        (r * cols + c, (r ^ row_bits) * cols + c // 4 * 4 + places[c % 4]) for r in range(rows) for c in range(cols)
    ]
    return lax.ppermute(x, ("rows", "cols"), pairs)


def powers(top):
    found = []
    while top > 1:
        top //= 2
        found.append(top)
    return found


def local(mesh_shape, points, lengthscale, target, probes, noise):
    features, width = points.shape
    rows, cols = mesh_shape
    vectors = probes.shape[0] + 1
    height = features + vectors
    packed_rows = width // LANES * height + height // 2
    block, base, packed = pl.pallas_call(
        prepare_kernel,
        out_shape=(
            VMEM((height, width), jnp.bfloat16),
            VMEM((vectors, width), jnp.float32),
            VMEM((packed_rows, LANES), jnp.bfloat16),
        ),
        in_specs=[IN_VMEM] * 5,
        out_specs=(IN_VMEM,) * 3,
    )(points, lengthscale[None, :], target[None, :], probes, noise[None, :])
    one = packed[None]
    for step in [(1, bits) for bits in powers(cols)[:-2]] + [(bits + 1, 0) for bits in powers(rows)[:-2]]:
        one = jnp.concatenate([one, swap(one, mesh_shape, *step)], axis=0)
    peer = swap(block, mesh_shape, 3, 0)
    next_to = swap(one, mesh_shape, 1, 1)
    ahead = turn(one, mesh_shape, 0, (2, 3, 1, 0))
    behind = turn(one, mesh_shape, 1, (3, 2, 0, 1))
    early = jnp.concatenate([one, ahead], axis=0)
    late = jnp.concatenate([next_to, behind], axis=0)
    total = add(features, [early], block, base)
    sent, total = lax.optimization_barrier((early, total))
    early_other = swap(sent, mesh_shape, 1, 0)
    late_other = swap(late, mesh_shape, 1, 0)
    partial = add(features, [early, early_other, late], peer)
    partial = add(features, [late_other], peer, partial)
    total = add(features, [early_other, late, late_other], block, total)
    return total + swap(partial, mesh_shape, 3, 0)


def solution(mesh):
    mesh_shape = (mesh.shape["rows"], mesh.shape["cols"])
    return jax.shard_map(
        functools.partial(local, mesh_shape),
        mesh=mesh,
        in_specs=(
            P(None, ("groups", "rows", "cols")),
            P("groups"),
            P(("groups", "rows", "cols")),
            P(None, ("groups", "rows", "cols")),
            P(("groups", "rows", "cols")),
        ),
        out_specs=P(None, ("groups", "rows", "cols")),
        check_vma=False,
    )
```

```python
import functools

import jax
import jax.numpy as jnp
from jax import lax
from jax.experimental import pallas as pl
from jax.experimental.pallas import tpu as pltpu
from jax.sharding import PartitionSpec as P

VMEM = pltpu.VMEM
IN_VMEM = pl.BlockSpec(memory_space=VMEM)
LANES = 128
CHUNK = 2
AHEAD = 2


def near(x):
    return pltpu.with_memory_space_constraint(x, VMEM)


def prepare_kernel(points_ref, lengthscale_ref, target_ref, probes_ref, noise_ref, scaled_ref, base_ref, packed_ref):
    features = points_ref.shape[0]
    wide = jnp.broadcast_to(lengthscale_ref[...], (features, features))
    row = lax.broadcasted_iota(jnp.int32, wide.shape, 0)
    col = lax.broadcasted_iota(jnp.int32, wide.shape, 1)
    scale = jnp.sum(jnp.where(row == col, wide, 0.0), axis=1, keepdims=True)
    scaled = points_ref[...] / scale
    signs = (2 * probes_ref[...] - 1).astype(jnp.float32)
    block = jnp.concatenate([scaled, target_ref[...], signs], axis=0)
    rows, width = block.shape
    full = width // LANES * LANES
    for tile in range(full // LANES):
        packed_ref[rows * tile : rows * (tile + 1), :] = block[:, LANES * tile : LANES * (tile + 1)].astype(jnp.bfloat16)
    high, low = block[: rows // 2, full:], block[rows // 2 :, full:]
    packed_ref[full // LANES * rows :, :] = jnp.concatenate([high, low, high, low], axis=1).astype(jnp.bfloat16)
    block = block.astype(jnp.bfloat16)
    scaled_ref[...] = block[:features]
    base_ref[...] = noise_ref[...] * block[features:].astype(jnp.float32)


def augmented(block, features, own):
    x = block.astype(jnp.float32)
    if own:
        x = jnp.concatenate([x, jnp.zeros((8, x.shape[1]), jnp.float32)], axis=0)
    row = lax.broadcasted_iota(jnp.int32, x.shape, 0)
    x = jnp.where(row < features, x, 0.0)
    half = -0.5 * jnp.sum(x * x, axis=0, keepdims=True)
    high = half.astype(jnp.bfloat16).astype(jnp.float32)
    rest = half - high
    middle = rest.astype(jnp.bfloat16).astype(jnp.float32)
    parts = [high, middle, rest - middle]
    rows = [1.0, 1.0, 1.0] + parts if own else parts + [1.0, 1.0, 1.0]
    for place, value in enumerate(rows):
        x = jnp.where(row == features + place, value, x)
    return x.astype(jnp.bfloat16)


def rest_tile(rests, features):
    quarter = LANES // 4
    rows = rests[0].shape[0]
    rests = [rest.astype(jnp.float32) for rest in rests]
    place = lax.broadcasted_iota(jnp.int32, (rows, LANES), 1) // quarter
    halves = [
        rests[at] if at + 1 >= len(rests) else jnp.where(place < 2, rests[at], rests[at + 1])
        for at in range(0, len(rests), 2)
    ]
    high, low = halves[0], pltpu.roll(halves[0], LANES - quarter, 1)
    if len(halves) == 2:
        high = jnp.where(place % 2 == 0, high, pltpu.roll(halves[1], quarter, 1))
        low = jnp.where(place % 2 == 0, low, halves[1])
    row = rows + lax.broadcasted_iota(jnp.int32, (rows, LANES), 0)
    for at, spot in enumerate((0, 2, 1, 3)):
        if at >= len(rests):
            low = jnp.where((place == spot) & (row >= features), 0.0, low)
    return jnp.concatenate([high, low], axis=0).astype(jnp.bfloat16)


def add_blocks(features, counts, *refs):
    piece_refs = refs[: len(counts)]
    own_ref, out_ref = refs[len(counts)], refs[-1]
    total = refs[len(counts) + 1][...] if len(refs) == len(counts) + 3 else None
    own_side = augmented(own_ref[...], features, True)
    rows = features + out_ref.shape[0]
    low = features // 16 * 16
    blocks = [(ref, k) for ref, count in zip(piece_refs, counts) for k in range(count)]
    whole = piece_refs[0].shape[1] // rows * rows
    tiles = [(ref, k, lo) for ref, k in blocks for lo in range(0, whole, rows)]
    tiles += [(blocks[at : at + 4],) for at in range(0, len(blocks), 4)]
    chunks = [tiles[at : at + CHUNK] for at in range(0, len(tiles), CHUNK)]

    def load(tile):
        if len(tile) == 3:
            ref, k, lo = tile
            return ref[k, lo : lo + rows, :]
        return rest_tile([ref[k, whole:, :] for ref, k in tile[0]], features)

    def exponent(chunk):
        block = jnp.concatenate([load(tile) for tile in chunk], axis=1)
        side = augmented(block, features, False)
        return block[low:], lax.dot_general(
            side, own_side, (((0,), (0,)), ((), ())), preferred_element_type=jnp.float32
        )

    found = total
    ahead = [exponent(chunk) for chunk in chunks[:AHEAD]]
    for step in range(len(chunks)):
        vectors, now = ahead.pop(0)
        if step + AHEAD < len(chunks):
            ahead.append(exponent(chunks[step + AHEAD]))
        kernel = jnp.exp(now).astype(jnp.bfloat16)
        term = jnp.dot(vectors, kernel, preferred_element_type=jnp.float32)
        term = term[features - low :]
        found = term if found is None else found + term
    out_ref[...] = found


def add(vectors, pieces, own, total=None):
    features, width = own.shape
    counts = tuple(piece.shape[0] for piece in pieces)
    operands = [near(x) for x in (*pieces, own, total) if x is not None]
    shape = (vectors, width)
    out = VMEM(shape, jnp.float32)
    work = sum(counts) * width * width
    return pl.pallas_call(
        functools.partial(add_blocks, features, counts),
        out_shape=out,
        in_specs=[IN_VMEM] * len(operands),
        out_specs=IN_VMEM,
        cost_estimate=pl.CostEstimate(flops=20480 * work, bytes_accessed=0, transcendentals=work),
    )(*operands)


def swap(x, mesh_shape, row_bits, col_bits):
    rows, cols = mesh_shape
    pairs = [
        (r * cols + c, (r ^ row_bits) * cols + (c ^ col_bits)) for r in range(rows) for c in range(cols)
    ]
    return lax.ppermute(x, ("rows", "cols"), pairs)


def turn(x, mesh_shape, row_bits, places):
    rows, cols = mesh_shape
    pairs = [
        (r * cols + c, (r ^ row_bits) * cols + c // 4 * 4 + places[c % 4]) for r in range(rows) for c in range(cols)
    ]
    return lax.ppermute(x, ("rows", "cols"), pairs)


def powers(top):
    found = []
    while top > 1:
        top //= 2
        found.append(top)
    return found


def local(mesh_shape, points, lengthscale, target, probes, noise):
    features, width = points.shape
    rows, cols = mesh_shape
    vectors = probes.shape[0] + 1
    height = features + vectors
    packed_rows = width // LANES * height + height // 2
    scaled, base, packed = pl.pallas_call(
        prepare_kernel,
        out_shape=(
            VMEM((features, width), jnp.bfloat16),
            VMEM((vectors, width), jnp.float32),
            VMEM((packed_rows, LANES), jnp.bfloat16),
        ),
        in_specs=[IN_VMEM] * 5,
        out_specs=(IN_VMEM,) * 3,
    )(points, lengthscale[None, :], target[None, :], probes, noise[None, :])
    one = packed[None]
    for step in [(1, bits) for bits in powers(cols)[:-2]] + [(bits + 1, 0) for bits in powers(rows)[:-2]]:
        one = jnp.concatenate([one, swap(one, mesh_shape, *step)], axis=0)
    peer = swap(scaled, mesh_shape, 3, 0)
    next_to = swap(one, mesh_shape, 1, 1)
    ahead = turn(one, mesh_shape, 0, (2, 3, 1, 0))
    behind = turn(one, mesh_shape, 1, (3, 2, 0, 1))
    early = jnp.concatenate([one, ahead], axis=0)
    late = jnp.concatenate([next_to, behind], axis=0)
    total = add(vectors, [early], scaled, base)
    sent, total = lax.optimization_barrier((early, total))
    early_other = swap(sent, mesh_shape, 1, 0)
    late_other = swap(late, mesh_shape, 1, 0)
    partial = add(vectors, [early, early_other, late], peer)
    partial = add(vectors, [late_other], peer, partial)
    total = add(vectors, [early_other, late, late_other], scaled, total)
    return total + swap(partial, mesh_shape, 3, 0)


def solution(mesh):
    mesh_shape = (mesh.shape["rows"], mesh.shape["cols"])
    return jax.shard_map(
        functools.partial(local, mesh_shape),
        mesh=mesh,
        in_specs=(
            P(None, ("groups", "rows", "cols")),
            P("groups"),
            P(("groups", "rows", "cols")),
            P(None, ("groups", "rows", "cols")),
            P(("groups", "rows", "cols")),
        ),
        out_specs=P(None, ("groups", "rows", "cols")),
        check_vma=False,
    )
```

```python
import functools

import jax
import jax.numpy as jnp
from jax import lax
from jax.experimental import pallas as pl
from jax.experimental.pallas import tpu as pltpu
from jax.sharding import PartitionSpec as P

VMEM = pltpu.VMEM
IN_VMEM = pl.BlockSpec(memory_space=VMEM)
LANES = 128
CHUNK = 2
AHEAD = 3


def near(x):
    return pltpu.with_memory_space_constraint(x, VMEM)


def prepare_kernel(points_ref, lengthscale_ref, target_ref, probes_ref, noise_ref, block_ref, base_ref, packed_ref):
    features = points_ref.shape[0]
    wide = jnp.broadcast_to(lengthscale_ref[...], (features, features))
    row = lax.broadcasted_iota(jnp.int32, wide.shape, 0)
    col = lax.broadcasted_iota(jnp.int32, wide.shape, 1)
    scale = jnp.sum(jnp.where(row == col, wide, 0.0), axis=1, keepdims=True)
    scaled = points_ref[...] / scale
    signs = (2 * probes_ref[...] - 1).astype(jnp.float32)
    block = jnp.concatenate([scaled, target_ref[...], signs], axis=0)
    rows, width = block.shape
    full = width // LANES * LANES
    for tile in range(full // LANES):
        packed_ref[rows * tile : rows * (tile + 1), :] = block[:, LANES * tile : LANES * (tile + 1)].astype(jnp.bfloat16)
    high, low = block[: rows // 2, full:], block[rows // 2 :, full:]
    packed_ref[full // LANES * rows :, :] = jnp.concatenate([high, low, high, low], axis=1).astype(jnp.bfloat16)
    block = block.astype(jnp.bfloat16)
    block_ref[...] = block
    base_ref[...] = noise_ref[...] * block[features:].astype(jnp.float32)


def augmented(block, features, own):
    x = block[:features].astype(jnp.float32)
    half = -0.5 * jnp.sum(x * x, axis=0, keepdims=True)
    high = half.astype(jnp.bfloat16).astype(jnp.float32)
    rest = half - high
    middle = rest.astype(jnp.bfloat16).astype(jnp.float32)
    row = lax.broadcasted_iota(jnp.int32, (8, x.shape[1]), 0)
    below = jnp.where(row < 6, 1.0, 0.0)
    for place, value in enumerate([high, middle, rest - middle], 3 if own else 0):
        below = jnp.where(row == place, value, below)
    return jnp.concatenate([x, below], axis=0).astype(jnp.bfloat16)


def rest_tile(rests, features):
    quarter = LANES // 4
    rows = rests[0].shape[0]
    rests = [rest.astype(jnp.float32) for rest in rests]
    place = lax.broadcasted_iota(jnp.int32, (rows, LANES), 1) // quarter
    halves = [
        rests[at] if at + 1 >= len(rests) else jnp.where(place < 2, rests[at], rests[at + 1])
        for at in range(0, len(rests), 2)
    ]
    high, low = halves[0], pltpu.roll(halves[0], LANES - quarter, 1)
    if len(halves) == 2:
        high = jnp.where(place % 2 == 0, high, pltpu.roll(halves[1], quarter, 1))
        low = jnp.where(place % 2 == 0, low, halves[1])
    row = rows + lax.broadcasted_iota(jnp.int32, (rows, LANES), 0)
    for at, spot in enumerate((0, 2, 1, 3)):
        if at >= len(rests):
            low = jnp.where((place == spot) & (row >= features), 0.0, low)
    return jnp.concatenate([high, low], axis=0).astype(jnp.bfloat16)


def add_blocks(features, counts, *refs):
    piece_refs = refs[: len(counts)]
    own_ref, out_ref = refs[len(counts)], refs[-1]
    total = refs[len(counts) + 1][...] if len(refs) == len(counts) + 3 else None
    own_side = augmented(own_ref[...], features, True)
    rows = own_ref.shape[0]
    low = features // 16 * 16
    blocks = [(ref, k) for ref, count in zip(piece_refs, counts) for k in range(count)]
    whole = piece_refs[0].shape[1] // rows * rows
    tiles = [(ref, k, lo) for ref, k in blocks for lo in range(0, whole, rows)]
    tiles += [(blocks[at : at + 4],) for at in range(0, len(blocks), 4)]
    chunks = [tiles[at : at + CHUNK] for at in range(0, len(tiles), CHUNK)]

    def load(tile):
        if len(tile) == 3:
            ref, k, lo = tile
            return ref[k, lo : lo + rows, :]
        return rest_tile([ref[k, whole:, :] for ref, k in tile[0]], features)

    def exponent(chunk):
        block = jnp.concatenate([load(tile) for tile in chunk], axis=1)
        side = augmented(block, features, False)
        return block[low:], lax.dot_general(
            side, own_side, (((0,), (0,)), ((), ())), preferred_element_type=jnp.float32
        )

    found = total
    ahead = [exponent(chunk) for chunk in chunks[:AHEAD]]
    for step in range(len(chunks)):
        vectors, now = ahead.pop(0)
        if step + AHEAD < len(chunks):
            ahead.append(exponent(chunks[step + AHEAD]))
        kernel = jnp.exp(now).astype(jnp.bfloat16)
        term = jnp.dot(vectors, kernel, preferred_element_type=jnp.float32)
        term = term[features - low :]
        found = term if found is None else found + term
    out_ref[...] = found


def add(features, pieces, own, total=None):
    rows, width = own.shape
    counts = tuple(piece.shape[0] for piece in pieces)
    operands = [near(x) for x in (*pieces, own, total) if x is not None]
    shape = (rows - features, width)
    out = VMEM(shape, jnp.float32)
    work = sum(counts) * width * width
    return pl.pallas_call(
        functools.partial(add_blocks, features, counts),
        out_shape=out,
        in_specs=[IN_VMEM] * len(operands),
        out_specs=IN_VMEM,
        cost_estimate=pl.CostEstimate(flops=20480 * work, bytes_accessed=0, transcendentals=work),
    )(*operands)


def swap(x, mesh_shape, row_bits, col_bits):
    rows, cols = mesh_shape
    pairs = [
        (r * cols + c, (r ^ row_bits) * cols + (c ^ col_bits)) for r in range(rows) for c in range(cols)
    ]
    return lax.ppermute(x, ("rows", "cols"), pairs)


def turn(x, mesh_shape, row_bits, places):
    rows, cols = mesh_shape
    pairs = [
        (r * cols + c, (r ^ row_bits) * cols + c // 4 * 4 + places[c % 4]) for r in range(rows) for c in range(cols)
    ]
    return lax.ppermute(x, ("rows", "cols"), pairs)


def powers(top):
    found = []
    while top > 1:
        top //= 2
        found.append(top)
    return found


def local(mesh_shape, points, lengthscale, target, probes, noise):
    features, width = points.shape
    rows, cols = mesh_shape
    vectors = probes.shape[0] + 1
    height = features + vectors
    packed_rows = width // LANES * height + height // 2
    block, base, packed = pl.pallas_call(
        prepare_kernel,
        out_shape=(
            VMEM((height, width), jnp.bfloat16),
            VMEM((vectors, width), jnp.float32),
            VMEM((packed_rows, LANES), jnp.bfloat16),
        ),
        in_specs=[IN_VMEM] * 5,
        out_specs=(IN_VMEM,) * 3,
    )(points, lengthscale[None, :], target[None, :], probes, noise[None, :])
    one = packed[None]
    for step in [(1, bits) for bits in powers(cols)[:-2]] + [(bits + 1, 0) for bits in powers(rows)[:-2]]:
        one = jnp.concatenate([one, swap(one, mesh_shape, *step)], axis=0)
    peer = swap(block, mesh_shape, 3, 0)
    next_to = swap(one, mesh_shape, 1, 1)
    ahead = turn(one, mesh_shape, 0, (2, 3, 1, 0))
    behind = turn(one, mesh_shape, 1, (3, 2, 0, 1))
    early = jnp.concatenate([one, ahead], axis=0)
    late = jnp.concatenate([next_to, behind], axis=0)
    total = add(features, [early], block, base)
    sent, total = lax.optimization_barrier((early, total))
    early_other = swap(sent, mesh_shape, 1, 0)
    late_other = swap(late, mesh_shape, 1, 0)
    partial = add(features, [early, early_other, late], peer)
    partial = add(features, [late_other], peer, partial)
    total = add(features, [early_other, late, late_other], block, total)
    return total + swap(partial, mesh_shape, 3, 0)


def solution(mesh):
    mesh_shape = (mesh.shape["rows"], mesh.shape["cols"])
    return jax.shard_map(
        functools.partial(local, mesh_shape),
        mesh=mesh,
        in_specs=(
            P(None, ("groups", "rows", "cols")),
            P("groups"),
            P(("groups", "rows", "cols")),
            P(None, ("groups", "rows", "cols")),
            P(("groups", "rows", "cols")),
        ),
        out_specs=P(None, ("groups", "rows", "cols")),
        check_vma=False,
    )
```

```python
import functools

import jax
import jax.numpy as jnp
from jax import lax
from jax.experimental import pallas as pl
from jax.experimental.pallas import tpu as pltpu
from jax.sharding import PartitionSpec as P

VMEM = pltpu.VMEM
IN_VMEM = pl.BlockSpec(memory_space=VMEM)
LANES = 128
CHUNK = 2
AHEAD = 2


def near(x):
    return pltpu.with_memory_space_constraint(x, VMEM)


def prepare_kernel(points_ref, lengthscale_ref, target_ref, probes_ref, noise_ref, block_ref, base_ref, packed_ref):
    features = points_ref.shape[0]
    wide = jnp.broadcast_to(lengthscale_ref[...], (features, features))
    row = lax.broadcasted_iota(jnp.int32, wide.shape, 0)
    col = lax.broadcasted_iota(jnp.int32, wide.shape, 1)
    scale = jnp.sum(jnp.where(row == col, wide, 0.0), axis=1, keepdims=True)
    scaled = points_ref[...] / scale
    signs = (2 * probes_ref[...] - 1).astype(jnp.float32)
    block = jnp.concatenate([scaled, target_ref[...], signs], axis=0)
    rows, width = block.shape
    full = width // LANES * LANES
    for tile in range(full // LANES):
        packed_ref[rows * tile : rows * (tile + 1), :] = block[:, LANES * tile : LANES * (tile + 1)].astype(jnp.bfloat16)
    high, low = block[: rows // 2, full:], block[rows // 2 :, full:]
    packed_ref[full // LANES * rows :, :] = jnp.concatenate([high, low, high, low], axis=1).astype(jnp.bfloat16)
    block = block.astype(jnp.bfloat16)
    block_ref[...] = block
    base_ref[...] = noise_ref[...] * block[features:].astype(jnp.float32)


def augmented(block, features, own):
    x = block.astype(jnp.float32)
    row = lax.broadcasted_iota(jnp.int32, x.shape, 0)
    x = jnp.where(row < features, x, 0.0)
    half = -0.5 * jnp.sum(x * x, axis=0, keepdims=True)
    high = half.astype(jnp.bfloat16).astype(jnp.float32)
    rest = half - high
    middle = rest.astype(jnp.bfloat16).astype(jnp.float32)
    parts = [high, middle, rest - middle]
    rows = [1.0, 1.0, 1.0] + parts if own else parts + [1.0, 1.0, 1.0]
    for place, value in enumerate(rows):
        x = jnp.where(row == features + place, value, x)
    return x.astype(jnp.bfloat16)


def rest_tile(rests, features):
    quarter = LANES // 4
    rows = rests[0].shape[0]
    rests = [rest.astype(jnp.float32) for rest in rests]
    place = lax.broadcasted_iota(jnp.int32, (rows, LANES), 1) // quarter
    halves = [
        rests[at] if at + 1 >= len(rests) else jnp.where(place < 2, rests[at], rests[at + 1])
        for at in range(0, len(rests), 2)
    ]
    high, low = halves[0], pltpu.roll(halves[0], LANES - quarter, 1)
    if len(halves) == 2:
        high = jnp.where(place % 2 == 0, high, pltpu.roll(halves[1], quarter, 1))
        low = jnp.where(place % 2 == 0, low, halves[1])
    row = rows + lax.broadcasted_iota(jnp.int32, (rows, LANES), 0)
    for at, spot in enumerate((0, 2, 1, 3)):
        if at >= len(rests):
            low = jnp.where((place == spot) & (row >= features), 0.0, low)
    return jnp.concatenate([high, low], axis=0).astype(jnp.bfloat16)


def add_blocks(features, counts, *refs):
    piece_refs = refs[: len(counts)]
    own_ref, out_ref = refs[len(counts)], refs[-1]
    total = refs[len(counts) + 1][...] if len(refs) == len(counts) + 3 else None
    own_side = augmented(own_ref[...], features, True)
    rows = own_ref.shape[0]
    low = features // 16 * 16
    blocks = [(ref, k) for ref, count in zip(piece_refs, counts) for k in range(count)]
    whole = piece_refs[0].shape[1] // rows * rows
    tiles = [(ref, k, lo) for ref, k in blocks for lo in range(0, whole, rows)]
    tiles += [(blocks[at : at + 4],) for at in range(0, len(blocks), 4)]
    chunks = [tiles[at : at + CHUNK] for at in range(0, len(tiles), CHUNK)]

    def load(tile):
        if len(tile) == 3:
            ref, k, lo = tile
            return ref[k, lo : lo + rows, :]
        return rest_tile([ref[k, whole:, :] for ref, k in tile[0]], features)

    def exponent(chunk):
        block = jnp.concatenate([load(tile) for tile in chunk], axis=1)
        side = augmented(block, features, False)
        return block[low:], lax.dot_general(
            side, own_side, (((0,), (0,)), ((), ())), preferred_element_type=jnp.float32
        )

    found = total
    ahead = [exponent(chunk) for chunk in chunks[:AHEAD]]
    for step in range(len(chunks)):
        vectors, now = ahead.pop(0)
        if step + AHEAD < len(chunks):
            ahead.append(exponent(chunks[step + AHEAD]))
        kernel = jnp.exp(now).astype(jnp.bfloat16)
        term = jnp.dot(vectors, kernel, preferred_element_type=jnp.float32)
        term = term[features - low :]
        found = term if found is None else found + term
    out_ref[...] = found


def add(features, pieces, own, total=None):
    rows, width = own.shape
    counts = tuple(piece.shape[0] for piece in pieces)
    operands = [near(x) for x in (*pieces, own, total) if x is not None]
    shape = (rows - features, width)
    out = VMEM(shape, jnp.float32)
    work = sum(counts) * width * width
    return pl.pallas_call(
        functools.partial(add_blocks, features, counts),
        out_shape=out,
        in_specs=[IN_VMEM] * len(operands),
        out_specs=IN_VMEM,
        cost_estimate=pl.CostEstimate(flops=20480 * work, bytes_accessed=0, transcendentals=work),
    )(*operands)


def swap(x, mesh_shape, row_bits, col_bits):
    rows, cols = mesh_shape
    pairs = [
        (r * cols + c, (r ^ row_bits) * cols + (c ^ col_bits)) for r in range(rows) for c in range(cols)
    ]
    return lax.ppermute(x, ("rows", "cols"), pairs)


def turn(x, mesh_shape, crossed, places):
    rows, cols = mesh_shape
    pairs = [
        (r * cols + c, (r ^ crossed[c % 4]) * cols + c // 4 * 4 + places[c % 4]) for r in range(rows) for c in range(cols)
    ]
    return lax.ppermute(x, ("rows", "cols"), pairs)


def powers(top):
    found = []
    while top > 1:
        top //= 2
        found.append(top)
    return found


def local(mesh_shape, points, lengthscale, target, probes, noise):
    features, width = points.shape
    rows, cols = mesh_shape
    vectors = probes.shape[0] + 1
    height = features + vectors
    packed_rows = width // LANES * height + height // 2
    block, base, packed = pl.pallas_call(
        prepare_kernel,
        out_shape=(
            VMEM((height, width), jnp.bfloat16),
            VMEM((vectors, width), jnp.float32),
            VMEM((packed_rows, LANES), jnp.bfloat16),
        ),
        in_specs=[IN_VMEM] * 5,
        out_specs=(IN_VMEM,) * 3,
    )(points, lengthscale[None, :], target[None, :], probes, noise[None, :])
    one = packed[None]
    for step in [(1, bits) for bits in powers(cols)[:-2]] + [(bits + 1, 0) for bits in powers(rows)[:-2]]:
        one = jnp.concatenate([one, swap(one, mesh_shape, *step)], axis=0)
    peer = swap(block, mesh_shape, 3, 0)
    next_to = turn(one, mesh_shape, (1, 1, 1, 1), (1, 0, 3, 2))
    ahead = turn(one, mesh_shape, (0, 0, 1, 0), (2, 3, 1, 0))
    behind = turn(one, mesh_shape, (1, 1, 1, 1), (3, 2, 0, 1))
    early = jnp.concatenate([one, ahead], axis=0)
    late = jnp.concatenate([next_to, behind], axis=0)
    total = add(features, [early], block, base)
    sent, total = lax.optimization_barrier((early, total))
    early_other = swap(sent, mesh_shape, 1, 0)
    late_other = swap(late, mesh_shape, 1, 0)
    partial = add(features, [early, early_other, late], peer)
    partial = add(features, [late_other], peer, partial)
    total = add(features, [early_other, late, late_other], block, total)
    return total + swap(partial, mesh_shape, 3, 0)


def solution(mesh):
    mesh_shape = (mesh.shape["rows"], mesh.shape["cols"])
    return jax.shard_map(
        functools.partial(local, mesh_shape),
        mesh=mesh,
        in_specs=(
            P(None, ("groups", "rows", "cols")),
            P("groups"),
            P(("groups", "rows", "cols")),
            P(None, ("groups", "rows", "cols")),
            P(("groups", "rows", "cols")),
        ),
        out_specs=P(None, ("groups", "rows", "cols")),
        check_vma=False,
    )
```
